32 devices in a mesh: grp: 2 (over x), seq: 8 (over z, y), chan: 2 (over core).
Axes of the slice: x: 2, y: 2, z: 4, core: 2. Of those that a mesh axis runs over, the one named last changes fastest.
Arguments:
- inputs: bfloat16 [262144, 768], P(('grp', 'seq'), 'chan'), parts along dimension 0, may hold values from -6 to 6
- cotangent: bfloat16 [262144, 768], P(('grp', 'seq'), 'chan'), parts along dimension 0, may hold values from -6 to 6
- conv_weight: float32 [2, 4, 768], P(None, None, 'chan'), may hold values from -3 to 3
- mix_inner: bfloat16 [256, 256], replicated, may hold values from -0.375 to 0.375
- twiddle: float32 [512, 256], P('seq'), may hold values from 0.5 to 2
- mix_outer: bfloat16 [512, 512], replicated, may hold values from -0.25 to 0.25
- proj_weight: bfloat16 [768, 768], P(None, 'chan'), may hold values from -0.21875 to 0.21875
Outputs:
- input_grad: bfloat16 [262144, 768], P(('grp', 'seq'), 'chan'), parts along dimension 0
- proj_grad: bfloat16 [1536, 768], P('grp', 'chan'), parts along dimension 0
- inner_grad: float32 [512, 256], P('grp'), parts along dimension 0
- outer_grad: float32 [1024, 512], P('grp'), parts along dimension 0
- conv_grad: float32 [4, 4, 768], P('grp', None, 'chan'), parts along dimension 0
The draws below stay inside these ranges and needn't reach their ends.
There are 2 independent parts, one for each index of `grp`. The reference program is written for one: setup_inputs(seed, part) draws one part's arguments, and reference() takes and returns one part's arrays. A program takes and returns all parts, laid end to end along the dimension named above; an argument that names none is the same for every part. Nothing has to cross between parts.
All inputs are finite; a program needn't handle non-finite values.
Results may differ from the reference program's by a relative error of at most 0.0067.
Values may be sent and summed in bfloat16 or wider, within the bound.
A program may use at most 448 MiB of HBM per device.

```python
import jax
import jax.numpy as jnp
from jax import lax

WIDTH = 768
INNER = 256
OUTER = 512
TAPS = 4
TOKENS = 131072


def level_of(own_key, shape, split, low, top_value):
    loudness = 1.0
    for position, shards_of in split:
        heights = jax.random.uniform(jax.random.fold_in(jax.random.fold_in(own_key, 6), position), (shards_of,), jnp.float32, low / len(split), top_value / len(split))
        loudness = loudness * jnp.repeat(jnp.exp(heights), shape[position] // shards_of).reshape((-1,) + (1,) * (len(shape) - 1 - position))
    return loudness


def centred(rng, dims, deviation, limit, shards=(), kind=jnp.bfloat16):
    factor_of = level_of(rng, dims, shards, -0.22, 0.18) if shards else 1.0
    values = jax.random.normal(rng, dims, jnp.float32) * deviation * factor_of
    return jnp.minimum(jnp.maximum(values, -limit), limit).astype(kind)


def setup_inputs(seed: int = 0, part: int = 0) -> dict:
    keys = jax.random.split(jax.random.key(seed), 8)
    own_keys = jax.random.split(jax.random.fold_in(keys[7], part), 8)
    inputs = centred(own_keys[0], (TOKENS, WIDTH), 1.0, 6.0, ((0, 8), (1, 2)))
    cotangent = centred(own_keys[1], (TOKENS, WIDTH), 1.0, 6.0, ((0, 8), (1, 2)))
    conv_weight = centred(keys[2], (2, TAPS, WIDTH), 0.5, 3.0, ((2, 2),), jnp.float32)
    mix_inner = centred(keys[3], (INNER, INNER), INNER ** -0.5, 0.375)
    twiddle = jnp.clip(0.5 + 1.5 * jax.random.uniform(keys[4], (OUTER, INNER), jnp.float32) ** level_of(keys[4], (OUTER, INNER), ((0, 8),), -0.2, 0.2), 0.5, 2.0)
    mix_outer = centred(keys[5], (OUTER, OUTER), OUTER ** -0.5, 0.25)
    proj_weight = centred(keys[6], (WIDTH, WIDTH), WIDTH ** -0.5, 0.21875, ((1, 2),))
    return dict(inputs=inputs, cotangent=cotangent, conv_weight=conv_weight, mix_inner=mix_inner, twiddle=twiddle, mix_outer=mix_outer, proj_weight=proj_weight)


def causal_taps(signal, weights):
    width_now = signal.shape[1]
    result = weights[0] * signal
    for offset in range(1, 4):
        delayed = jnp.concatenate([jnp.zeros((offset, width_now), jnp.float32), signal[:-offset]], 0)
        result = result + weights[offset] * delayed
    return result

def taps_ahead(signal, weights):
    width_now = signal.shape[1]
    result = weights[0] * signal
    for offset in range(1, 4):
        advanced = jnp.concatenate([signal[offset:], jnp.zeros((offset, width_now), jnp.float32)], 0)
        result = result + weights[offset] * advanced
    return result

def taps_grad(signal, source):
    totals = [lax.optimization_barrier(jnp.sum(signal * source, 0))]
    for offset in range(1, 4):
        totals.append(lax.optimization_barrier(jnp.sum(signal[offset:] * source[:-offset], 0)))
    return jnp.stack(totals)

def reference(inputs, cotangent, conv_weight, mix_inner, twiddle, mix_outer, proj_weight):
    signal = inputs.astype(jnp.float32)
    value_conv = causal_taps(signal, conv_weight[0])
    gate_conv = causal_taps(signal, conv_weight[1])
    gate_sig = jax.nn.sigmoid(gate_conv)
    gated_input = (value_conv * gate_sig).astype(jnp.bfloat16)
    gated_blocks = gated_input.reshape(OUTER, INNER, WIDTH)
    inner_weight = mix_inner.astype(jnp.float32)
    outer_weight = mix_outer.astype(jnp.float32)
    inner_mixed = jnp.einsum('kj,ijc->ikc', inner_weight, gated_blocks.astype(jnp.float32))
    twisted = (inner_mixed * twiddle[:, :, None]).astype(jnp.bfloat16)
    mixed_out = jnp.einsum('mi,ikc->mkc', outer_weight, twisted.astype(jnp.float32)).astype(jnp.bfloat16)
    mixed_rows = mixed_out.reshape(TOKENS, WIDTH)
    grad_scale = TOKENS ** (-0.5)
    proj_sum = jnp.dot(mixed_rows.T, cotangent, preferred_element_type=jnp.float32)
    mixed_grad = jnp.dot(cotangent, proj_weight.T, preferred_element_type=jnp.float32).astype(jnp.bfloat16)
    mixed_grad_blocks = mixed_grad.reshape(OUTER, INNER, WIDTH).astype(jnp.float32)
    twisted_grad = jnp.einsum('mi,mkc->ikc', outer_weight, mixed_grad_blocks).astype(jnp.bfloat16)
    outer_sum = jnp.einsum('mkc,ikc->mi', mixed_grad_blocks, twisted.astype(jnp.float32))
    inner_mixed_grad = (twisted_grad.astype(jnp.float32) * twiddle[:, :, None]).astype(jnp.bfloat16)
    inner_mixed_wide = inner_mixed_grad.astype(jnp.float32)
    gated_grad = jnp.einsum('kj,ikc->ijc', inner_weight, inner_mixed_wide).reshape(TOKENS, WIDTH)
    inner_sum = jnp.einsum('ikc,ijc->kj', inner_mixed_wide, gated_blocks.astype(jnp.float32))
    value_grad = gated_grad * gate_sig
    gate_grad = gated_grad * value_conv * gate_sig * (1.0 - gate_sig)
    input_grad = cotangent.astype(jnp.float32) + taps_ahead(value_grad, conv_weight[0]) + taps_ahead(gate_grad, conv_weight[1])
    conv_sum = jnp.stack([taps_grad(value_grad, signal), taps_grad(gate_grad, signal)])
    return (input_grad.astype(jnp.bfloat16), (proj_sum * grad_scale).astype(jnp.bfloat16), inner_sum * grad_scale, outer_sum * grad_scale, conv_sum * grad_scale)
```

```python
import functools

import jax
import jax.numpy as jnp
from jax import lax
from jax.experimental import pallas as pl
from jax.experimental.pallas import tpu as pltpu
from jax.sharding import PartitionSpec as P

CHUNKS = 3


def passed_along(array, axis, by):
    peers = lax.axis_size(axis)
    pairs = [(i, i + by) for i in range(peers) if 0 <= i + by < peers]
    return lax.ppermute(array, axis, pairs)


def causal_taps(history_rows, weights, tokens):
    result = weights[0] * history_rows[3 : 3 + tokens]
    for offset in range(1, 4):
        result = result + weights[offset] * history_rows[3 - offset : 3 - offset + tokens]
    return result


def exchange(blocks):
    peers = len(blocks)
    received = [blocks[0]]
    for step in range(1, peers):
        pairs = [(i, (i + step) % peers) for i in range(peers)]
        received.append(lax.ppermute(blocks[step], "seq", pairs))
    return received


def by_source(array, axis, peers, me):
    shape = array.shape
    size = shape[axis] // peers
    parts = [lax.slice_in_dim(array, b * size, (b + 1) * size, axis=axis) for b in range(peers)]
    backwards = jnp.concatenate(parts[::-1] * 2, axis)
    return lax.dynamic_slice_in_dim(backwards, (peers - 1 - me) * size, shape[axis], axis)


def by_target(array, axis, peers, me):
    size = array.shape[axis] // peers
    twice = jnp.concatenate([array, array], axis)
    return lax.dynamic_slice_in_dim(twice, me * size, array.shape[axis], axis)


def tail_kernel(
    parts, *refs
):
    grad_refs = refs[:parts]
    (inputs_ref, before_ref, last_ref, cot_ref, weight_ref, mix_ref, halo_ref) = refs[parts : parts + 7]
    (out_ref, inner_ref, conv_ref) = refs[-6:-3]
    (signal, value_ext, gate_ext) = refs[-3:]
    step = pl.program_id(0)
    steps = pl.num_programs(0)
    rows = inputs_ref.shape[0]
    taps = weight_ref.shape[1]

    @pl.when(step == 0)
    def _():
        inner_ref[...] = jnp.zeros_like(inner_ref)
        conv_ref[...] = jnp.zeros_like(conv_ref)
        value_ext[0:8] = halo_ref[0]
        gate_ext[0:8] = halo_ref[1]

    value_ext[rows : rows + 8] = value_ext[0:8]
    gate_ext[rows : rows + 8] = gate_ext[0:8]
    signal[8 : 8 + rows] = inputs_ref[...].astype(jnp.float32)
    before = before_ref[...].astype(jnp.float32)[8:16]
    signal[0:8] = jnp.where(step == steps - 1, last_ref[...], before)
    weight = weight_ref[...]
    shifted = [signal[8 - s : 8 - s + rows] for s in range(taps)]
    value_conv = weight[0, 0][None] * shifted[0]
    gate_conv = weight[1, 0][None] * shifted[0]
    for s in range(1, taps):
        value_conv = value_conv + weight[0, s][None] * shifted[s]
        gate_conv = gate_conv + weight[1, s][None] * shifted[s]
    gate_sig = jax.nn.sigmoid(gate_conv)
    value_part = value_conv * gate_sig
    gated = value_part.astype(jnp.bfloat16)
    if parts > 1:
        grad = jnp.concatenate([ref[0] for ref in grad_refs], 0)
    else:
        grad = grad_refs[0][0]
    inner_ref[...] += lax.dot_general(
        grad, gated, (((1,), (1,)), ((), ())), preferred_element_type=jnp.float32
    )
    gated_grad = jnp.dot(mix_ref[...], grad, preferred_element_type=jnp.float32)
    value_grad = gated_grad * gate_sig
    gate_grad = gated_grad * value_part * (1.0 - gate_sig)
    value_ext[0:rows] = value_grad
    gate_ext[0:rows] = gate_grad
    for s in range(taps):
        conv_ref[0, s] += jnp.sum((value_grad * shifted[s]).reshape(rows // 8, 8, -1), 0)
        conv_ref[1, s] += jnp.sum((gate_grad * shifted[s]).reshape(rows // 8, 8, -1), 0)
    total = cot_ref[...].astype(jnp.float32)
    for s in range(taps):
        total = total + weight[0, s][None] * value_ext[s : s + rows]
        total = total + weight[1, s][None] * gate_ext[s : s + rows]
    out_ref[...] = total.astype(jnp.bfloat16)


def tail(grads, inputs, last_rows, cotangent, conv_weight, mix_turned, halo, chunk, width, result):
    tokens, channels = inputs.shape
    inner_size = mix_turned.shape[0]
    blocks = tokens // inner_size
    parts = len(grads)

    def place(step):
        return blocks - 1 - step

    ratio = inner_size // 16
    in_specs = [
        pl.BlockSpec((1, g.shape[1], width), lambda step: (place(step), 0, 0)) for g in grads
    ] + [
        pl.BlockSpec((inner_size, width), lambda step: (place(step), chunk)),
        pl.BlockSpec((16, width), lambda step: (jnp.maximum(place(step) * ratio - 1, 0), chunk)),
        pl.BlockSpec((8, width), lambda step: (0, chunk)),
        pl.BlockSpec((inner_size, width), lambda step: (place(step), chunk)),
        pl.BlockSpec((2, 4, width), lambda step: (0, 0, chunk)),
        pl.BlockSpec((inner_size, inner_size), lambda step: (0, 0)),
        pl.BlockSpec((2, 8, width), lambda step: (0, 0, 0)),
    ]
    operands = [*grads, inputs, inputs, last_rows, cotangent, conv_weight, mix_turned, halo]
    aliases = {}
    if result is not None:
        aliases = {len(operands): 0}
        operands.append(result)
        in_specs.append(pl.BlockSpec(memory_space=pl.ANY))
    return pl.pallas_call(
        functools.partial(tail_kernel, parts),
        grid=(blocks,),
        in_specs=in_specs,
        out_specs=[
            pl.BlockSpec((inner_size, width), lambda step: (place(step), chunk)),
            pl.BlockSpec((inner_size, inner_size), lambda step: (0, 0)),
            pl.BlockSpec((2, 4, 8, width), lambda step: (0, 0, 0, 0)),
        ],
        out_shape=[
            jax.ShapeDtypeStruct((tokens, channels), jnp.bfloat16),
            jax.ShapeDtypeStruct((inner_size, inner_size), jnp.float32),
            jax.ShapeDtypeStruct((2, 4, 8, width), jnp.float32),
        ],
        scratch_shapes=[pltpu.VMEM((inner_size + 8, width), jnp.float32)] * 3,
        input_output_aliases=aliases,
        compiler_params=pltpu.CompilerParams(vmem_limit_bytes=32 * 1024 * 1024),
        cost_estimate=pl.CostEstimate(
            flops=tokens * width * inner_size * 16,
            bytes_accessed=tokens * width * 8,
            transcendentals=tokens * width,
        ),
    )(*operands)


def body(inputs, cotangent, conv_weight, mix_inner, twiddle, mix_outer, proj_weight):
    peers = lax.axis_size("seq")
    me = lax.axis_index("seq")
    half = lax.axis_index("chan")
    halves = lax.axis_size("chan")
    inner_size = mix_inner.shape[0]
    outer_size = mix_outer.shape[0]
    tokens, channels = inputs.shape
    blocks = tokens // inner_size
    cols = inner_size // peers
    grad_scale = (outer_size * inner_size) ** (-0.5)

    cot_blocks = cotangent.reshape(blocks, inner_size, channels)
    cot_sends = [
        lax.dynamic_slice_in_dim(cot_blocks, lax.rem(me + s, peers) * cols, cols, 1)
        for s in range(peers)
    ]
    cot_parts = exchange(cot_sends)
    last_rows = passed_along(inputs[tokens - 3 :], "seq", 1)
    twiddle_all = lax.all_gather(twiddle, "seq", axis=0, tiled=True)
    swap = [(i, halves - 1 - i) for i in range(halves)]
    weight_all = lax.all_gather(proj_weight, "chan", axis=1, tiled=True)
    weight_rows = lax.dynamic_slice_in_dim(weight_all, half * channels, channels, 0)

    history_rows = jnp.concatenate([last_rows, inputs], 0).astype(jnp.float32)
    value_conv = causal_taps(history_rows, conv_weight[0], tokens)
    gate_conv = causal_taps(history_rows, conv_weight[1], tokens)
    gated_input = (value_conv * jax.nn.sigmoid(gate_conv)).astype(jnp.bfloat16)
    gated_blocks = gated_input.reshape(blocks, inner_size, channels)
    mix_target = by_target(mix_inner, 0, peers, me)
    twiddle_target = by_target(twiddle, 1, peers, me)
    inner_mixed = jnp.einsum(
        "kj,ijc->ikc", mix_target, gated_blocks, preferred_element_type=jnp.float32
    )
    twisted = (inner_mixed * twiddle_target[:, :, None]).astype(jnp.bfloat16)
    twisted, cot_parts = lax.optimization_barrier((twisted, cot_parts))
    twisted_parts = exchange([twisted[:, s * cols : (s + 1) * cols] for s in range(peers)])

    cot_turned = jnp.concatenate(cot_parts, 0)
    cot_wide = lax.all_gather(cot_turned, "chan", axis=2, tiled=True)
    outer_rows = by_source(mix_outer, 0, peers, me)
    outer_target = by_target(outer_rows, 1, peers, me)
    twiddle_cols = lax.dynamic_slice_in_dim(twiddle_all, me * cols, cols, 1)
    twiddle_cols = by_target(twiddle_cols, 0, peers, me)
    mixed_grad = jnp.einsum(
        "mkd,cd->mkc", cot_wide, weight_rows, preferred_element_type=jnp.float32
    ).astype(jnp.bfloat16)
    width = channels // CHUNKS
    grad_parts = []
    for chunk in range(CHUNKS):
        piece = mixed_grad[:, :, chunk * width : (chunk + 1) * width]
        twisted_grad = jnp.einsum(
            "mi,mkc->ikc", outer_target, piece, preferred_element_type=jnp.float32
        ).astype(jnp.bfloat16)
        turned = (twisted_grad.astype(jnp.float32) * twiddle_cols[:, :, None]).astype(jnp.bfloat16)
        grad_parts.append(exchange([turned[s * blocks : (s + 1) * blocks] for s in range(peers)]))

    received = jnp.concatenate(twisted_parts, 0)
    outer_both = by_source(outer_rows, 1, peers, me)
    mixed = jnp.einsum(
        "mi,ikc->mkc", outer_both, received, preferred_element_type=jnp.float32
    ).astype(jnp.bfloat16)
    outer_part = jnp.einsum(
        "mkc,ikc->mi", mixed_grad, received, preferred_element_type=jnp.float32
    )
    outer_part = by_source(by_source(outer_part, 0, peers, me), 1, peers, me)
    proj_part = lax.dot_general(
        mixed.reshape(-1, channels),
        cot_wide.reshape(-1, channels * halves),
        (((0,), (0,)), ((), ())),
        preferred_element_type=jnp.float32,
    )
    own = lax.dynamic_slice_in_dim(proj_part, half * channels, channels, 1)
    other = lax.dynamic_slice_in_dim(proj_part, (halves - 1 - half) * channels, channels, 1)
    other = lax.ppermute(other, "chan", swap)
    proj_part = jnp.where(
        half == 0, jnp.concatenate([own, other], 0), jnp.concatenate([other, own], 0)
    )
    proj_sum = lax.psum(proj_part, "seq")
    outer_sum = lax.psum(outer_part, ("seq", "chan"))

    mix_source = by_source(mix_inner, 0, peers, me)
    mix_turned = mix_source.T
    pad_rows = jnp.concatenate([jnp.zeros((5, channels), jnp.bfloat16), last_rows], 0)
    pad_rows = pad_rows.astype(jnp.float32)
    first_history = jnp.concatenate([last_rows, inputs[:3]], 0).astype(jnp.float32)
    first_value = causal_taps(first_history, conv_weight[0], 3)
    first_sig = jax.nn.sigmoid(causal_taps(first_history, conv_weight[1], 3))
    result = None
    inner_part = 0.0
    conv_parts = []
    for chunk in range(CHUNKS):
        grads = grad_parts[chunk]
        lanes = slice(chunk * width, (chunk + 1) * width)
        first = jnp.concatenate([g[0] for g in grads], 0)
        first_grad = lax.dot_general(
            mix_source[:, :3], first, (((0,), (0,)), ((), ())), preferred_element_type=jnp.float32
        )
        sig = first_sig[:, lanes]
        edge = jnp.stack([first_grad * sig, first_grad * first_value[:, lanes] * sig * (1.0 - sig)])
        halo = passed_along(edge, "seq", -1)
        halo = jnp.concatenate([halo, jnp.zeros((2, 5, width), jnp.float32)], 1)
        if cols % 16:
            grads = [jnp.concatenate(grads, 1)]
        result, inner_one, conv_one = tail(
            grads, inputs, pad_rows, cotangent, conv_weight, mix_turned, halo, chunk, width, result
        )
        inner_part = inner_part + inner_one
        conv_parts.append(jnp.sum(conv_one, 2))
    inner_part = by_source(inner_part, 0, peers, me)
    conv_sum = lax.psum(jnp.concatenate(conv_parts, 2), "seq")
    inner_sum = lax.psum(inner_part, ("seq", "chan"))
    return (
        result,
        (proj_sum * grad_scale).astype(jnp.bfloat16),
        inner_sum * grad_scale,
        outer_sum * grad_scale,
        conv_sum * grad_scale,
    )


def solution(mesh):
    in_specs = (
        P(("grp", "seq"), "chan"),
        P(("grp", "seq"), "chan"),
        P(None, None, "chan"),
        P(),
        P("seq", None),
        P(),
        P(None, "chan"),
    )
    out_specs = (
        P(("grp", "seq"), "chan"),
        P("grp", "chan"),
        P("grp", None),
        P("grp", None),
        P("grp", None, "chan"),
    )
    return jax.shard_map(body, mesh=mesh, in_specs=in_specs, out_specs=out_specs, check_vma=False)
```

```python
import jax
import jax.numpy as jnp
from jax import lax
from jax.experimental import pallas as pl
from jax.experimental.pallas import tpu as pltpu
from jax.sharding import PartitionSpec as P


def passed_along(array, axis, by):
    peers = lax.axis_size(axis)
    pairs = [(i, i + by) for i in range(peers) if 0 <= i + by < peers]
    return lax.ppermute(array, axis, pairs)


def causal_taps(history_rows, weights, tokens):
    result = weights[0] * history_rows[3 : 3 + tokens]
    for offset in range(1, 4):
        result = result + weights[offset] * history_rows[3 - offset : 3 - offset + tokens]
    return result


def exchange(array):
    return lax.all_to_all(array, "seq", split_axis=0, concat_axis=0, tiled=True)


def tail_kernel(*refs):
    (grad_ref, twiddle_ref, inputs_ref, before_ref, last_ref) = refs[:5]
    (cot_ref, weight_ref, mix_ref, halo_ref) = refs[5:9]
    (out_ref, inner_ref, conv_ref) = refs[-6:-3]
    (signal, value_ext, gate_ext) = refs[-3:]
    step = pl.program_id(0)
    steps = pl.num_programs(0)
    rows = inputs_ref.shape[0]
    taps = weight_ref.shape[1]

    @pl.when(step == 0)
    def _():
        inner_ref[...] = jnp.zeros_like(inner_ref)
        conv_ref[...] = jnp.zeros_like(conv_ref)
        value_ext[0:8] = halo_ref[0]
        gate_ext[0:8] = halo_ref[1]

    value_ext[rows : rows + 8] = value_ext[0:8]
    gate_ext[rows : rows + 8] = gate_ext[0:8]
    signal[8 : 8 + rows] = inputs_ref[...].astype(jnp.float32)
    before = before_ref[...].astype(jnp.float32)[8:16]
    signal[0:8] = jnp.where(step == steps - 1, last_ref[...], before)
    weight = weight_ref[...]
    shifted = [signal[8 - s : 8 - s + rows] for s in range(taps)]
    value_conv = weight[0, 0][None] * shifted[0]
    gate_conv = weight[1, 0][None] * shifted[0]
    for s in range(1, taps):
        value_conv = value_conv + weight[0, s][None] * shifted[s]
        gate_conv = gate_conv + weight[1, s][None] * shifted[s]
    gate_sig = jax.nn.sigmoid(gate_conv)
    value_part = value_conv * gate_sig
    gated = value_part.astype(jnp.bfloat16)
    grad = grad_ref[:, 0].reshape(rows, -1).astype(jnp.float32)
    table = twiddle_ref[...]
    lane = lax.broadcasted_iota(jnp.int32, table.shape, 1)
    factor = jnp.sum(jnp.where(lane == steps - 1 - step, table, 0.0), 1, keepdims=True)
    grad = (grad * factor).astype(jnp.bfloat16)
    inner_ref[...] += lax.dot_general(
        grad, gated, (((1,), (1,)), ((), ())), preferred_element_type=jnp.float32
    )
    gated_grad = jnp.dot(mix_ref[...], grad, preferred_element_type=jnp.float32)
    value_grad = gated_grad * gate_sig
    gate_grad = gated_grad * value_part * (1.0 - gate_sig)
    value_ext[0:rows] = value_grad
    gate_ext[0:rows] = gate_grad
    for s in range(taps):
        conv_ref[0, s] += jnp.sum((value_grad * shifted[s]).reshape(rows // 8, 8, -1), 0)
        conv_ref[1, s] += jnp.sum((gate_grad * shifted[s]).reshape(rows // 8, 8, -1), 0)
    total = cot_ref[...].astype(jnp.float32)
    for s in range(taps):
        total = total + weight[0, s][None] * value_ext[s : s + rows]
        total = total + weight[1, s][None] * gate_ext[s : s + rows]
    out_ref[...] = total.astype(jnp.bfloat16)


def tail(grads, turned_twiddle, inputs, last_rows, cotangent, conv_weight, mix_turned, halo):
    tokens, channels = inputs.shape
    inner_size = mix_turned.shape[0]
    blocks = tokens // inner_size
    ratio = inner_size // 16

    def place(step):
        return blocks - 1 - step

    whole = pl.BlockSpec(memory_space=pltpu.VMEM)
    rows = pl.BlockSpec((inner_size, channels), lambda step: (place(step), 0))
    before = pl.BlockSpec(
        (16, channels), lambda step: (jnp.maximum(place(step) * ratio - 1, 0), 0)
    )
    grad_rows = pl.BlockSpec(
        (grads.shape[0], 1, grads.shape[2], channels), lambda step: (0, place(step), 0, 0)
    )
    return pl.pallas_call(
        tail_kernel,
        grid=(blocks,),
        in_specs=[grad_rows, whole, rows, before, whole, rows, whole, whole, whole],
        out_specs=[
            rows,
            pl.BlockSpec((inner_size, inner_size), lambda step: (0, 0)),
            pl.BlockSpec((2, 4, 8, channels), lambda step: (0, 0, 0, 0)),
        ],
        out_shape=[
            jax.ShapeDtypeStruct((tokens, channels), jnp.bfloat16),
            jax.ShapeDtypeStruct((inner_size, inner_size), jnp.float32),
            jax.ShapeDtypeStruct((2, 4, 8, channels), jnp.float32),
        ],
        scratch_shapes=[pltpu.VMEM((inner_size + 8, channels), jnp.float32)] * 3,
        compiler_params=pltpu.CompilerParams(vmem_limit_bytes=32 * 1024 * 1024),
        cost_estimate=pl.CostEstimate(
            flops=tokens * channels * inner_size * 4,
            bytes_accessed=tokens * channels * 8,
            transcendentals=tokens * channels,
        ),
    )(
        grads, turned_twiddle, inputs, inputs, last_rows, cotangent, conv_weight, mix_turned, halo
    )


def body(inputs, cotangent, conv_weight, mix_inner, twiddle, mix_outer, proj_weight):
    peers = lax.axis_size("seq")
    half = lax.axis_index("chan")
    halves = lax.axis_size("chan")
    inner_size = mix_inner.shape[0]
    outer_size = mix_outer.shape[0]
    tokens, channels = inputs.shape
    blocks = tokens // inner_size
    cols = inner_size // peers
    grad_scale = (outer_size * inner_size) ** (-0.5)
    swap = [(i, halves - 1 - i) for i in range(halves)]

    def by_owner(array):
        turned = array.reshape(blocks, peers, cols, channels).transpose(1, 0, 2, 3)
        return turned.reshape(peers * blocks, cols, channels)

    cot_turned = exchange(by_owner(cotangent))
    last_rows = passed_along(inputs[tokens - 3 :], "seq", 1)
    weight_all = lax.all_gather(proj_weight, "chan", axis=1)
    weight_rows = lax.dynamic_slice_in_dim(weight_all, half * channels, channels, 0)

    history_rows = jnp.concatenate([last_rows, inputs], 0).astype(jnp.float32)
    value_conv = causal_taps(history_rows, conv_weight[0], tokens)
    gate_conv = causal_taps(history_rows, conv_weight[1], tokens)
    gated_input = (value_conv * jax.nn.sigmoid(gate_conv)).astype(jnp.bfloat16)
    gated_blocks = gated_input.reshape(blocks, inner_size, channels)
    inner_mixed = jnp.einsum(
        "kj,ijc->ikc", mix_inner, gated_blocks, preferred_element_type=jnp.float32
    )
    twisted = (inner_mixed * twiddle[:, :, None]).astype(jnp.bfloat16)
    sent = by_owner(twisted)
    sent, cot_turned = lax.optimization_barrier((sent, cot_turned))
    received = exchange(sent)

    cot_wide = lax.all_gather(cot_turned, "chan", axis=0)
    mixed_grad = jnp.einsum(
        "hmkd,chd->mkc", cot_wide, weight_rows, preferred_element_type=jnp.float32
    ).astype(jnp.bfloat16)
    twisted_grad = jnp.einsum(
        "mi,mkc->ikc", mix_outer, mixed_grad, preferred_element_type=jnp.float32
    ).astype(jnp.bfloat16)
    twisted_grad, received = lax.optimization_barrier((twisted_grad, received))
    grads = exchange(twisted_grad).reshape(peers, blocks, cols, channels)

    mixed = jnp.einsum(
        "mi,ikc->mkc", mix_outer, received, preferred_element_type=jnp.float32
    ).astype(jnp.bfloat16)
    outer_part = jnp.einsum(
        "mkc,ikc->mi", mixed_grad, received, preferred_element_type=jnp.float32
    )
    proj_part = jnp.einsum(
        "mkc,hmkd->hcd", mixed, cot_wide, preferred_element_type=jnp.float32
    )
    own = lax.dynamic_index_in_dim(proj_part, half, 0, keepdims=False)
    other = lax.dynamic_index_in_dim(proj_part, halves - 1 - half, 0, keepdims=False)
    other, outer_other = lax.ppermute((other, outer_part), "chan", swap)
    proj_part = jnp.where(
        half == 0, jnp.concatenate([own, other], 0), jnp.concatenate([other, own], 0)
    )
    proj_sum, outer_sum = lax.psum((proj_part, outer_part + outer_other), "seq")

    pad_rows = jnp.concatenate([jnp.zeros((5, channels), jnp.bfloat16), last_rows], 0)
    pad_rows = pad_rows.astype(jnp.float32)
    first_history = jnp.concatenate([last_rows, inputs[:3]], 0).astype(jnp.float32)
    first_value = causal_taps(first_history, conv_weight[0], 3)
    sig = jax.nn.sigmoid(causal_taps(first_history, conv_weight[1], 3))
    first = grads[:, 0].reshape(inner_size, channels).astype(jnp.float32)
    first = (first * twiddle[0][:, None]).astype(jnp.bfloat16)
    first_grad = lax.dot_general(
        mix_inner[:, :3], first, (((0,), (0,)), ((), ())), preferred_element_type=jnp.float32
    )
    edge = jnp.stack([first_grad * sig, first_grad * first_value * sig * (1.0 - sig)])
    halo = passed_along(edge, "seq", -1)
    halo = jnp.concatenate([halo, jnp.zeros((2, 5, channels), jnp.float32)], 1)
    if cols % 16:
        grads = grads.transpose(1, 0, 2, 3).reshape(1, blocks, inner_size, channels)
    result, inner_part, conv_part = tail(
        grads, twiddle.T, inputs, pad_rows, cotangent, conv_weight, mix_inner.T, halo
    )
    conv_part = jnp.sum(conv_part, 2).reshape(1, -1)
    mine = (jnp.arange(halves) == half)[:, None]
    conv_both = jnp.where(mine, conv_part, 0.0)
    flat = jnp.concatenate([inner_part.reshape(-1), conv_both.reshape(-1)])
    flat = lax.psum(flat, ("seq", "chan"))
    inner_sum = flat[: inner_size * inner_size].reshape(inner_size, inner_size)
    conv_both = flat[inner_size * inner_size :].reshape(halves, *conv_weight.shape)
    conv_sum = lax.dynamic_index_in_dim(conv_both, half, 0, keepdims=False)
    return (
        result,
        (proj_sum * grad_scale).astype(jnp.bfloat16),
        inner_sum * grad_scale,
        outer_sum * grad_scale,
        conv_sum * grad_scale,
    )


def solution(mesh):
    in_specs = (
        P(("grp", "seq"), "chan"),
        P(("grp", "seq"), "chan"),
        P(None, None, "chan"),
        P(),
        P("seq", None),
        P(),
        P(None, "chan"),
    )
    out_specs = (
        P(("grp", "seq"), "chan"),
        P("grp", "chan"),
        P("grp", None),
        P("grp", None),
        P("grp", None, "chan"),
    )
    return jax.shard_map(body, mesh=mesh, in_specs=in_specs, out_specs=out_specs, check_vma=False)
```
